32 devices in a mesh: dp: 4 (over z), fsdp: 2 (over x), expert: 4 (over y, core).
Axes of the slice: x: 2, y: 2, z: 4, core: 2. Of those that a mesh axis runs over, the one named last changes fastest.
Arguments:
- tokens: bfloat16 [2048, 4096], P(('dp', 'expert'), 'fsdp'), may hold values from -6 to 6
- cotangent: bfloat16 [2048, 4096], P(('dp', 'expert'), 'fsdp'), may hold values from -6 to 6
- routes: int32 [2048, 8], P(('dp', 'expert')), may hold values from 0 to 127, as said below
- route_gates: float32 [2048, 8], P(('dp', 'expert')), may hold values from 0.05 to 0.6
- gate_weight: bfloat16 [4, 4096, 768], P('expert', None, 'fsdp'), may hold values from -0.09375 to 0.09375
- up_weight: bfloat16 [4, 4096, 768], P('expert', None, 'fsdp'), may hold values from -0.09375 to 0.09375
- down_weight: bfloat16 [4, 768, 4096], P('expert', 'fsdp'), may hold values from -0.21875 to 0.21875
Outputs:
- token_grads: bfloat16 [2048, 4096], P(('dp', 'expert'), 'fsdp')
- gate_grads: bfloat16 [4, 4096, 768], P('expert', 'dp', 'fsdp')
- up_grads: bfloat16 [4, 4096, 768], P('expert', 'dp', 'fsdp')
- down_grads: bfloat16 [4, 768, 4096], P('expert', 'fsdp', 'dp')
The draws below stay inside these ranges and needn't reach their ends.
Inputs may be any that keep to these rules, and one draw needn't show every extreme that they name: `routes`: each token names 8 different ids, exactly one in each run of 16 ids (0 to 15, 16 to 31, and so on). In each aligned block of 128 tokens (one index of dp and expert together) no id below 16 is named by more than 10 tokens, and in every draw one id below 4 is named by exactly 10 tokens of every block.
All inputs are finite; a program needn't handle non-finite values.
Results may differ from the reference program's by a relative error of at most 0.017.
Values may be sent and summed in bfloat16 or wider, within the bound.
A program may use at most 64 MiB of HBM per device.

```python
import jax
import jax.numpy as jnp
from jax import lax

D = 4096
TOPK = 8
FF_WIN = 768
TOK = 128
GROUP = 16
CAP = 10
EXPERTS = 4
TOKENS = 2048
N_DP = 4
N_FSDP = 2
N_EXPERT = 4


def draw_routes(key, part):
    keys = jax.random.split(key, 4)
    favored = jax.random.randint(keys[0], (), 0, EXPERTS)
    pooled = ((jnp.arange(GROUP * CAP, dtype=jnp.int32) // CAP + favored) % GROUP).astype(jnp.int32)

    def one_block(block_key):
        first_key, second_key = jax.random.split(block_key)
        others = jax.random.permutation(first_key, pooled[CAP:])
        chosen = jnp.concatenate([pooled[:CAP], others[:TOK - CAP]])
        return jax.random.permutation(second_key, chosen)
    window_ids = jax.vmap(one_block)(jax.random.split(keys[1], TOKENS // TOK)).reshape(TOKENS)
    spare = jax.random.randint(keys[2], (TOKENS, TOPK), 0, GROUP)
    scores = jax.random.randint(keys[3], (TOKENS, TOPK), 0, 1048576) * TOPK + jnp.arange(TOPK, dtype=jnp.int32)[None, :]
    groups = jnp.argsort(scores, axis=1).astype(jnp.int32)
    local_ids = jnp.where(groups == 0, window_ids[:, None], spare)
    return (groups * GROUP + local_ids).astype(jnp.int32)


def raised(array, stream_key, source, target, shards_of, factor):
    def block_of(position):
        return (jnp.arange(array.shape[position]) // (array.shape[position] // shards_of)).reshape((-1,) + (1,) * (array.ndim - 1 - position))

    one_side = jax.random.permutation(stream_key, shards_of)[block_of(target)]
    second = (block_of(target) + shards_of // 2) % shards_of
    return jnp.where((block_of(source) == one_side) | (block_of(source) == second), factor * array, array)


def levels(own_key, dims, pieces, least, high):
    gain, own = 1.0, jax.random.fold_in(own_key, 6)
    for position, shards_of in pieces:
        heights = jnp.exp(jax.random.uniform(jax.random.fold_in(own, position), (shards_of,), jnp.float32, least / len(pieces), high / len(pieces)))
        gain = gain * jnp.repeat(heights, dims[position] // shards_of).reshape([-1 if axis == position else 1 for axis in range(len(dims))])
    return gain


def bell_draw(stream_key, dims, deviation, most, shards=(), kind=jnp.bfloat16):
    values = jax.random.normal(stream_key, dims, jnp.float32) * deviation
    if len(shards) > 0:
        values = levels(stream_key, dims, shards, -0.22, 0.18) * values
    return jnp.clip(values, min=-most, max=most).astype(kind)


def bell_draw_with(rng, dims, deviation, limit, pieces, heavy, kind=jnp.bfloat16):
    array = deviation * jax.random.normal(rng, dims, jnp.float32)
    if pieces:
        array = array * levels(rng, dims, pieces, -0.22, 0.18)
    return jnp.clip(raised(array, jax.random.fold_in(rng, 3), *heavy), -limit, limit).astype(kind)


def setup_inputs(seed: int = 0) -> dict:
    streams_of = jax.random.split(jax.random.key(seed), 8)
    tokens = bell_draw_with(streams_of[0], (TOKENS, D), 1.0, 6.0, ((0, 16), (1, 2)), (0, 1, 16, 2.0))
    cotangent = bell_draw(streams_of[1], (TOKENS, D), 1.0, 6.0, ((0, 16), (1, 2)))
    routes = draw_routes(jax.random.fold_in(streams_of[7], 71), 0)
    route_gates = jnp.clip(0.05 + 0.55 * jax.random.uniform(streams_of[3], (TOKENS, TOPK), jnp.float32) ** levels(streams_of[3], (TOKENS, TOPK), ((0, 16),), -0.2, 0.2), 0.05, 0.6)
    gate_weight = bell_draw(streams_of[4], (EXPERTS, D, FF_WIN), D ** -0.5, 0.09375, ((0, 4), (2, 2)))
    up_weight = bell_draw(streams_of[5], (EXPERTS, D, FF_WIN), D ** -0.5, 0.09375, ((0, 4), (2, 2)))
    down_weight = bell_draw(streams_of[6], (EXPERTS, FF_WIN, D), FF_WIN ** -0.5, 0.21875, ((0, 4), (1, 2)))
    return {"tokens": tokens, "cotangent": cotangent, "routes": routes, "route_gates": route_gates, "gate_weight": gate_weight, "up_weight": up_weight, "down_weight": down_weight}


def reference(tokens, cotangent, routes, route_gates, gate_weight, up_weight, down_weight):
    in_window = routes < EXPERTS
    target = jnp.where(jnp.any(in_window, axis=1), jnp.sum(jnp.where(in_window, routes, 0), axis=1), EXPERTS).astype(jnp.int32)
    route_gate = jnp.sum(jnp.where(in_window, route_gates, jnp.float32(0.0)), axis=1)
    scaled = (route_gate[:, None] * cotangent.astype(jnp.float32)).astype(jnp.bfloat16)
    group_rows = TOK * N_EXPERT
    slot_count = CAP * N_EXPERT
    block_width = FF_WIN // N_FSDP
    padding = jnp.zeros((1, D), jnp.bfloat16)
    grouped_rows = tokens.reshape(N_DP, group_rows, D)
    grouped_grads = scaled.reshape(N_DP, group_rows, D)
    grouped_target = target.reshape(N_DP, group_rows)

    def per_expert(expert_id):
        gate_mat = gate_weight[expert_id]
        up_mat = up_weight[expert_id]
        down_mat = down_weight[expert_id]

        def per_group(running, group_id):
            row_index = jnp.nonzero(grouped_target[group_id] == expert_id, size=slot_count, fill_value=group_rows)[0].astype(jnp.int32)
            rows_in = jnp.concatenate([grouped_rows[group_id], padding], axis=0)[row_index]
            grads_in = jnp.concatenate([grouped_grads[group_id], padding], axis=0)[row_index]
            gate_pre = jnp.dot(rows_in, gate_mat, preferred_element_type=jnp.float32)
            up_pre = jnp.dot(rows_in, up_mat, preferred_element_type=jnp.float32)
            sigmoid_gate = jax.nn.sigmoid(gate_pre)
            activated = gate_pre * sigmoid_gate
            hidden = (activated * up_pre).astype(jnp.bfloat16)
            hidden_grad = jnp.dot(grads_in, down_mat.T, preferred_element_type=jnp.float32)
            gate_grad = (hidden_grad * up_pre * sigmoid_gate * (1.0 + gate_pre * (1.0 - sigmoid_gate))).astype(jnp.bfloat16)
            up_grad = (hidden_grad * activated).astype(jnp.bfloat16)
            row_sum = jnp.zeros((slot_count, D), jnp.float32)
            for column_block in range(N_FSDP):
                column_low = column_block * block_width
                column_high = column_low + block_width
                block_term = jnp.dot(gate_grad[:, column_low:column_high], gate_mat[:, column_low:column_high].T, preferred_element_type=jnp.float32)
                block_term = block_term + jnp.dot(up_grad[:, column_low:column_high], up_mat[:, column_low:column_high].T, preferred_element_type=jnp.float32)
                rounded = lax.optimization_barrier(block_term.astype(jnp.bfloat16))
                row_sum = row_sum + rounded.astype(jnp.float32)
            term_gate = jnp.dot(rows_in.T, gate_grad, preferred_element_type=jnp.float32).astype(jnp.bfloat16)
            term_up = jnp.dot(rows_in.T, up_grad, preferred_element_type=jnp.float32).astype(jnp.bfloat16)
            term_down = jnp.dot(hidden.T, grads_in, preferred_element_type=jnp.float32).astype(jnp.bfloat16)
            term_gate, term_up, term_down = lax.optimization_barrier((term_gate, term_up, term_down))
            running = (running[0] + term_gate.astype(jnp.float32), running[1] + term_up.astype(jnp.float32), running[2] + term_down.astype(jnp.float32))
            row_place = jnp.where(row_index < group_rows, row_index + group_id * group_rows, TOKENS).astype(jnp.int32)
            return running, (row_sum.astype(jnp.bfloat16), row_place)

        initial = (jnp.zeros((D, FF_WIN), jnp.float32), jnp.zeros((D, FF_WIN), jnp.float32), jnp.zeros((FF_WIN, D), jnp.float32))
        running, outputs = lax.scan(per_group, initial, jnp.arange(N_DP, dtype=jnp.int32))
        return running[0].astype(jnp.bfloat16), running[1].astype(jnp.bfloat16), running[2].astype(jnp.bfloat16), outputs[0], outputs[1]

    gate_grads, up_grads, down_grads, rows_out, places = lax.map(per_expert, jnp.arange(EXPERTS, dtype=jnp.int32))
    token_grads = jnp.zeros((TOKENS, D), jnp.bfloat16).at[places.reshape(-1)].set(rows_out.reshape(-1, D), mode="drop")
    return token_grads, gate_grads, up_grads, down_grads
```

```python
import jax
import jax.numpy as jnp
from jax import lax
from jax.sharding import PartitionSpec as P

CAP = 10


def local(tokens, cotangent, routes, route_gates, gate_weight, up_weight, down_weight):
    owners = lax.axis_size("expert")
    quarter = tokens.shape[1]
    in_window = routes < owners
    target = jnp.where(
        jnp.any(in_window, axis=1), jnp.sum(jnp.where(in_window, routes, 0), axis=1), owners
    )
    route_gate = jnp.sum(jnp.where(in_window, route_gates, jnp.float32(0.0)), axis=1)
    scaled = (route_gate[:, None] * cotangent.astype(jnp.float32)).astype(jnp.bfloat16)
    onehot = (target[:, None] == jnp.arange(owners, dtype=jnp.int32)[None, :]).astype(jnp.int32)
    before = jnp.cumsum(onehot, axis=0) - onehot
    position = target * CAP + jnp.sum(before * onehot, axis=1)
    slot_count = owners * CAP
    selector = (jnp.arange(slot_count, dtype=jnp.int32)[:, None] == position[None, :]).astype(
        jnp.bfloat16
    )
    send_rows = (
        jnp.dot(selector, tokens, preferred_element_type=jnp.float32)
        .astype(jnp.bfloat16)
        .reshape(owners, CAP, quarter)
    )
    send_grads = (
        jnp.dot(selector, scaled, preferred_element_type=jnp.float32)
        .astype(jnp.bfloat16)
        .reshape(owners, CAP, quarter)
    )
    recv_rows, recv_grads = (
        lax.all_to_all(send_rows, "expert", split_axis=0, concat_axis=0, tiled=True),
        lax.all_to_all(send_grads, "expert", split_axis=0, concat_axis=0, tiled=True),
    )
    flat_rows = recv_rows.reshape(slot_count, quarter)
    flat_grads = recv_grads.reshape(slot_count, quarter)
    full_rows, full_grads = (
        lax.all_gather(flat_rows, "fsdp", axis=1, tiled=True),
        lax.all_gather(flat_grads, "fsdp", axis=1, tiled=True),
    )
    gate_mat = gate_weight[0]
    up_mat = up_weight[0]
    down_mat = down_weight[0]
    across = (((1,), (1,)), ((), ()))
    gate_pre = jnp.dot(full_rows, gate_mat, preferred_element_type=jnp.float32)
    up_pre = jnp.dot(full_rows, up_mat, preferred_element_type=jnp.float32)
    sigmoid_gate = jax.nn.sigmoid(gate_pre)
    activated = gate_pre * sigmoid_gate
    hidden = (activated * up_pre).astype(jnp.bfloat16)
    hidden_grad = lax.dot_general(full_grads, down_mat, across, preferred_element_type=jnp.float32)
    gate_grad = (
        hidden_grad * up_pre * sigmoid_gate * (1.0 + gate_pre * (1.0 - sigmoid_gate))
    ).astype(jnp.bfloat16)
    up_grad = (hidden_grad * activated).astype(jnp.bfloat16)
    partial_value = lax.dot_general(gate_grad, gate_mat, across, preferred_element_type=jnp.float32)
    partial_value = partial_value + lax.dot_general(
        up_grad, up_mat, across, preferred_element_type=jnp.float32
    )
    route_rows = lax.psum_scatter(
        partial_value.astype(jnp.bfloat16), "fsdp", scatter_dimension=1, tiled=True
    )
    returned = lax.all_to_all(
        route_rows.reshape(owners, CAP, quarter), "expert", split_axis=0, concat_axis=0, tiled=True
    )
    token_grads = lax.dot_general(
        selector,
        returned.reshape(slot_count, quarter),
        (((0,), (0,)), ((), ())),
        preferred_element_type=jnp.float32,
    ).astype(jnp.bfloat16)
    contract = (((0,), (0,)), ((), ()))
    block_width = gate_mat.shape[1]
    groups = lax.axis_size("dp")
    slices = jnp.concatenate([full_rows, full_grads], axis=0).reshape(
        2 * slot_count, groups, -1
    )
    slices = lax.all_to_all(slices, "dp", split_axis=1, concat_axis=1, tiled=True)
    slices = slices.reshape(2, slot_count, groups, -1)
    factors = lax.all_gather(
        jnp.concatenate([gate_grad, up_grad, hidden], axis=1), "dp", axis=1, tiled=False
    )
    many = slot_count * groups
    rows_slice = slices[0].reshape(many, -1)
    grads_slice = slices[1].reshape(many, -1)
    factors = factors.reshape(many, -1)
    gate_up = lax.dot_general(
        rows_slice, factors[:, : 2 * block_width], contract, preferred_element_type=jnp.float32
    ).astype(jnp.bfloat16)
    gate_grads = gate_up[:, :block_width][None]
    up_grads = gate_up[:, block_width:][None]
    down_grads = lax.dot_general(
        factors[:, 2 * block_width :], grads_slice, contract, preferred_element_type=jnp.float32
    ).astype(jnp.bfloat16)[None]
    return (token_grads, gate_grads, up_grads, down_grads)


def solution(mesh):
    placed = (
        P(("dp", "expert"), "fsdp"),
        P(("dp", "expert"), "fsdp"),
        P(("dp", "expert"), None),
        P(("dp", "expert"), None),
        P("expert", None, "fsdp"),
        P("expert", None, "fsdp"),
        P("expert", "fsdp", None),
    )
    return jax.shard_map(
        local,
        mesh=mesh,
        in_specs=placed,
        out_specs=(
            P(("dp", "expert"), "fsdp"),
            P("expert", "dp", "fsdp"),
            P("expert", "dp", "fsdp"),
            P("expert", "fsdp", "dp"),
        ),
        check_vma=False,
    )
```

```python
import functools

import jax
import jax.numpy as jnp
import numpy as np
from jax import lax
from jax.experimental import pallas as pl
from jax.experimental.pallas import tpu as pltpu
from jax.sharding import PartitionSpec as P

CAP = 10
OUT_FOLD = 4
BACK_FOLD = 8
ROWS = 2 * CAP * OUT_FOLD
STRIDE = 4096.0
MESH = pl.DeviceIdType.MESH
F32 = jnp.float32
BF16 = jnp.bfloat16


def dot(a, b, ca=1, cb=0):
    return lax.dot_general(a, b, (((ca,), (cb,)), ((), ())), preferred_element_type=F32)


def kernel(
    groups, halves, owners,
    tokens, cotangent, routes, route_gates, gate_hbm, up_hbm, down_hbm, out_key, back_key, unpack, permute,
    token_grads, gate_grads, up_grads, down_grads,
    gate_w, up_w, down_w, packed, landed, rows_all, slices, mine, factors, back, returned,
    w_sem, send1, recv1, send2, recv2, send3, recv3, send4, recv4,
):
    g, f, e = lax.axis_index("dp"), lax.axis_index("fsdp"), lax.axis_index("expert")
    slots = owners * CAP
    quarter = tokens.shape[1]
    width = quarter // OUT_FOLD
    back_width = quarter // BACK_FOLD
    ff = gate_w.shape[1]
    part = slices.shape[2]
    plane = [(a, b) for a in range(halves) for b in range(owners) if (a, b) != (0, 0)]
    far = lambda a, b: (lax.rem(f + a, halves), lax.rem(e + b, owners))

    loads = [
        pltpu.make_async_copy(src.at[0], dst, w_sem.at[i])
        for i, (src, dst) in enumerate(((gate_hbm, gate_w), (up_hbm, up_w), (down_hbm, down_w)))
    ]
    for load in loads:
        load.start()

    barrier = pltpu.get_barrier_semaphore()
    for a, b in plane:
        pf, pe = far(a, b)
        pl.semaphore_signal(barrier, inc=1, device_id=(g, pf, pe), device_id_type=MESH)
    for k in range(1, groups):
        pl.semaphore_signal(
            barrier, inc=1, device_id=(lax.rem(g + k, groups), f, e), device_id_type=MESH
        )

    count = tokens.shape[0]
    ids = routes[...].astype(F32)
    inside = ids < float(owners)
    target = jnp.sum(jnp.where(inside, ids, 0.0), axis=1, keepdims=True)
    named = jnp.sum(jnp.where(inside, 1.0, 0.0), axis=1, keepdims=True)
    target = jnp.where(named > 0.0, target, float(owners))
    route_gate = jnp.sum(jnp.where(inside, route_gates[...], 0.0), axis=1, keepdims=True)
    scaled = (route_gate * cotangent[...].astype(F32)).astype(BF16)
    lanes = lax.broadcasted_iota(jnp.int32, (count, count), 1)
    subs = lax.broadcasted_iota(jnp.int32, (count, count), 0)
    onehot = jnp.where(lanes.astype(F32) == target, 1.0, 0.0)
    earlier = jnp.where(lanes < subs, 1.0, 0.0).astype(BF16)
    before = dot(earlier, onehot.astype(BF16))
    position = target * float(CAP) + jnp.sum(before * onehot, axis=1, keepdims=True)
    across = jnp.sum(jnp.where(lanes == subs, position, 0.0), axis=0, keepdims=True)

    key = out_key[...]
    picks, stacked = [], []
    for chunk in range(OUT_FOLD):
        for which, source in enumerate((tokens[...], scaled)):
            offset = STRIDE * (2 * chunk + which)
            picks.append(jnp.where(key == across + offset, 1.0, 0.0).astype(BF16))
            stacked.append(source[:, chunk * width : (chunk + 1) * width])
    sent = dot(jnp.concatenate(picks, axis=1), jnp.concatenate(stacked, axis=0))
    packed[...] = sent.astype(BF16).reshape(packed.shape)

    pl.semaphore_wait(barrier, len(plane) + groups - 1)
    outs = []
    for i, (a, b) in enumerate(plane):
        pf, pe = far(a, b)
        copy = pltpu.make_async_remote_copy(
            packed.at[pe], landed.at[f * owners + e], send1.at[i], recv1.at[f * owners + e],
            device_id=(g, pf, pe), device_id_type=MESH,
        )
        copy.start()
        outs.append(copy)
    landed[f * owners + e] = packed[e]

    for i, (a, b) in enumerate(plane):
        pf, pe = far(a, b)
        pltpu.make_async_remote_copy(
            packed.at[pe], landed.at[pf * owners + pe], send1.at[i], recv1.at[pf * owners + pe],
            device_id=(g, pf, pe), device_id_type=MESH,
        ).wait_recv()
    for half in range(halves):
        block = landed[half * owners : (half + 1) * owners].reshape(owners * ROWS, width)
        for chunk in range(OUT_FOLD):
            low = half * quarter + chunk * width
            rows_all[:, low : low + width] = dot(unpack[chunk], block).astype(BF16)
    for k in range(1, groups):
        d = lax.rem(g + k, groups)
        copy = pltpu.make_async_remote_copy(
            rows_all.at[:, pl.ds(pl.multiple_of(d * part, part), part)], slices.at[g],
            send2.at[k - 1], recv2.at[g], device_id=(d, f, e), device_id_type=MESH,
        )
        copy.start()
        outs.append(copy)
    slices[g] = rows_all[:, pl.ds(pl.multiple_of(g * part, part), part)]

    for load in loads:
        load.wait()
    full = rows_all[...]
    gate_pre = dot(full, gate_w[...])[:slots]
    up_pre = dot(full, up_w[...])[:slots]
    hidden_grad = dot(full, down_w[...], 1, 1)[slots:]
    sigmoid_gate = jax.nn.sigmoid(gate_pre)
    activated = gate_pre * sigmoid_gate
    hidden = activated * up_pre
    gate_grad = hidden_grad * up_pre * sigmoid_gate * (1.0 + gate_pre * (1.0 - sigmoid_gate))
    up_grad = hidden_grad * activated
    mine[...] = jnp.concatenate(
        [
            jnp.concatenate([gate_grad, up_grad], axis=1),
            jnp.concatenate([hidden, jnp.zeros_like(hidden)], axis=1),
        ],
        axis=0,
    ).astype(BF16)
    for k in range(1, groups):
        d = lax.rem(g + k, groups)
        copy = pltpu.make_async_remote_copy(
            mine, factors.at[g], send3.at[k - 1], recv3.at[g],
            device_id=(d, f, e), device_id_type=MESH,
        )
        copy.start()
        outs.append(copy)
    factors[g] = mine[...]

    gate_grad, up_grad = gate_grad.astype(BF16), up_grad.astype(BF16)
    for half in range(halves):
        terms = []
        for chunk in range(BACK_FOLD):
            low = half * quarter + chunk * back_width
            term = dot(gate_grad, gate_w[low : low + back_width, :], 1, 1)
            terms.append(term + dot(up_grad, up_w[low : low + back_width, :], 1, 1))
        ordered = dot(permute[...], jnp.concatenate(terms, axis=0).astype(BF16))
        back[half * owners : (half + 1) * owners] = ordered.astype(BF16).reshape(
            owners, ROWS, back_width
        )
    for i, (a, b) in enumerate(plane):
        pf, pe = far(a, b)
        copy = pltpu.make_async_remote_copy(
            back.at[pf * owners + pe], returned.at[f * owners + e], send4.at[i],
            recv4.at[f * owners + e], device_id=(g, pf, pe), device_id_type=MESH,
        )
        copy.start()
        outs.append(copy)
    returned[f * owners + e] = back[f * owners + e]

    for i, (a, b) in enumerate(plane):
        pf, pe = far(a, b)
        pltpu.make_async_remote_copy(
            back.at[pf * owners + pe], returned.at[pf * owners + pe], send4.at[i],
            recv4.at[pf * owners + pe], device_id=(g, pf, pe), device_id_type=MESH,
        ).wait_recv()
    come = returned[...].reshape(halves * owners * ROWS, back_width)
    place = jnp.broadcast_to(position, (count, back_key.shape[1]))
    for chunk in range(BACK_FOLD):
        pick = jnp.where(place + STRIDE * chunk == back_key[...], 1.0, 0.0).astype(BF16)
        low = chunk * back_width
        token_grads[:, low : low + back_width] = dot(pick, come).astype(BF16)

    for k in range(1, groups):
        d = lax.rem(g + k, groups)
        pltpu.make_async_remote_copy(
            rows_all.at[:, pl.ds(0, part)], slices.at[d], send2.at[k - 1], recv2.at[d],
            device_id=(d, f, e), device_id_type=MESH,
        ).wait_recv()
        pltpu.make_async_remote_copy(
            mine, factors.at[d], send3.at[k - 1], recv3.at[d],
            device_id=(d, f, e), device_id_type=MESH,
        ).wait_recv()
    many = groups * 2 * slots
    every = slices[...].reshape(many, part)
    top = lax.broadcasted_iota(jnp.int32, (groups, 2 * slots, ff), 1) < slots
    held = factors[...].astype(F32)
    low, high = held[:, :, :ff], held[:, :, ff:]
    for value, wanted, out in ((low, True, gate_grads), (high, True, up_grads)):
        value = jnp.where(top, value, 0.0).astype(BF16).reshape(many, ff)
        out[0] = dot(every, value, 0, 0).astype(BF16)
    value = jnp.where(top, 0.0, low).astype(BF16).reshape(many, ff)
    down_grads[0] = dot(value, every, 0, 0).astype(BF16)
    for copy in outs:
        copy.wait_send()


def local(groups, halves, owners, tokens, cotangent, routes, route_gates, gate_weight, up_weight, down_weight):
    quarter = tokens.shape[1]
    model, ff = gate_weight.shape[1:]
    slots = owners * CAP
    count = tokens.shape[0]
    part = model // groups
    width, back_width = quarter // OUT_FOLD, quarter // BACK_FOLD

    at = np.arange(owners * ROWS)
    owner, chunk = at // ROWS, at % ROWS // (2 * CAP)
    which, row = at % (2 * CAP) // CAP, at % CAP
    out_key = (owner * CAP + row + STRIDE * (2 * chunk + which)).astype(np.float32)
    out_key = np.broadcast_to(out_key[:, None], (owners * ROWS, count))
    spot = which * slots + owner * CAP + row
    unpack = np.stack([
        (spot[None, :] == np.arange(2 * slots)[:, None]) & (chunk == c)[None, :]
        for c in range(OUT_FOLD)
    ])
    back_chunk = at % ROWS // CAP
    slot = owner * CAP + row
    permute = (back_chunk * slots + slot)[:, None] == np.arange(BACK_FOLD * slots)[None, :]
    back_key = np.tile((slot + STRIDE * back_chunk).astype(np.float32), halves)[None, :]

    vmem = pl.BlockSpec(memory_space=pltpu.VMEM)
    anywhere = pl.BlockSpec(memory_space=pl.ANY)
    peers = halves * owners
    dma = pltpu.SemaphoreType.DMA
    return pl.pallas_call(
        functools.partial(kernel, groups, halves, owners),
        out_shape=(
            jax.ShapeDtypeStruct((count, quarter), BF16),
            jax.ShapeDtypeStruct((1, part, ff), BF16),
            jax.ShapeDtypeStruct((1, part, ff), BF16),
            jax.ShapeDtypeStruct((1, ff, part), BF16),
        ),
        in_specs=[vmem] * 4 + [anywhere] * 3 + [vmem] * 4,
        out_specs=(vmem,) * 4,
        scratch_shapes=[
            pltpu.VMEM((model, ff), BF16),
            pltpu.VMEM((model, ff), BF16),
            pltpu.VMEM((ff, model), BF16),
            pltpu.VMEM((owners, ROWS, width), BF16),
            pltpu.VMEM((peers, ROWS, width), BF16),
            pltpu.VMEM((2 * slots, model), BF16),
            pltpu.VMEM((groups, 2 * slots, part), BF16),
            pltpu.VMEM((2 * slots, 2 * ff), BF16),
            pltpu.VMEM((groups, 2 * slots, 2 * ff), BF16),
            pltpu.VMEM((peers, ROWS, back_width), BF16),
            pltpu.VMEM((peers, ROWS, back_width), BF16),
            dma((3,)),
            dma((peers,)),
            dma((peers,)),
            dma((groups,)),
            dma((groups,)),
            dma((groups,)),
            dma((groups,)),
            dma((peers,)),
            dma((peers,)),
        ],
        compiler_params=pltpu.CompilerParams(
            collective_id=0, has_side_effects=True, vmem_limit_bytes=56 * 1024 * 1024
        ),
    )(
        tokens, cotangent, routes, route_gates, gate_weight, up_weight, down_weight,
        jnp.asarray(out_key), jnp.asarray(back_key), jnp.asarray(unpack, BF16), jnp.asarray(permute, BF16),
    )


def solution(mesh):
    placed = (
        P(("dp", "expert"), "fsdp"),
        P(("dp", "expert"), "fsdp"),
        P(("dp", "expert"), None),
        P(("dp", "expert"), None),
        P("expert", None, "fsdp"),
        P("expert", None, "fsdp"),
        P("expert", "fsdp", None),
    )
    sizes = (mesh.shape["dp"], mesh.shape["fsdp"], mesh.shape["expert"])
    return jax.shard_map(
        functools.partial(local, *sizes),
        mesh=mesh,
        in_specs=placed,
        out_specs=(
            P(("dp", "expert"), "fsdp"),
            P("expert", "dp", "fsdp"),
            P("expert", "dp", "fsdp"),
            P("expert", "fsdp", "dp"),
        ),
        check_vma=False,
    )
```

```python
import functools

import jax
import jax.numpy as jnp
import numpy as np
from jax import lax
from jax.experimental import pallas as pl
from jax.experimental.pallas import tpu as pltpu
from jax.sharding import PartitionSpec as P

CAP = 10
OUT_FOLD = 4
BACK_FOLD = 8
ROWS = 2 * CAP * OUT_FOLD
STRIDE = 4096.0
MESH = pl.DeviceIdType.MESH
F32 = jnp.float32
BF16 = jnp.bfloat16


def dot(a, b, ca=1, cb=0):
    return lax.dot_general(a, b, (((ca,), (cb,)), ((), ())), preferred_element_type=F32)


def place(routes, owners):
    ids = routes.astype(F32)
    inside = ids < float(owners)
    target = jnp.sum(jnp.where(inside, ids, 0.0), axis=0, keepdims=True)
    named = jnp.sum(jnp.where(inside, 1.0, 0.0), axis=0, keepdims=True)
    target = jnp.where(named > 0.0, target, float(owners))
    count = routes.shape[1]
    lanes = lax.broadcasted_iota(jnp.int32, (count, count), 1)
    subs = lax.broadcasted_iota(jnp.int32, (count, count), 0)
    onehot = jnp.where(subs.astype(F32) == target, 1.0, 0.0)
    earlier = jnp.where(subs < lanes, 1.0, 0.0).astype(BF16)
    before = dot(onehot.astype(BF16), earlier)
    position = target * float(CAP) + jnp.sum(before * onehot, axis=0, keepdims=True)
    return inside, position, lanes == subs


def column(row, diagonal):
    return jnp.sum(jnp.where(diagonal, row, 0.0), axis=1, keepdims=True)


def folded(shape, axis):
    at = lax.broadcasted_iota(jnp.int32, shape, axis).astype(F32)
    owner = jnp.floor((at + 0.5) * (1.0 / ROWS))
    at = at - owner * ROWS
    fold = jnp.floor((at + 0.5) * (1.0 / CAP))
    return owner * CAP + (at - fold * CAP), fold


def kernel(
    groups, halves, owners,
    tokens, cotangent, routes, route_gates, gate_hbm, up_hbm, down_hbm,
    slices, factors, returned,
    gate_w, up_w, down_w, packed, landed, rows_all, mine, back,
    w_sem, send1, recv1, send2, recv2, send3, recv3, send4, recv4, send5, recv5,
):
    g, f, e = lax.axis_index("dp"), lax.axis_index("fsdp"), lax.axis_index("expert")
    slots = owners * CAP
    quarter = tokens.shape[1]
    width = quarter // OUT_FOLD
    back_width = quarter // BACK_FOLD
    part = slices.shape[2]
    plane = [(a, b) for a in range(halves) for b in range(owners) if (a, b) != (0, 0)]
    far = lambda a, b: (lax.rem(f + a, halves), lax.rem(e + b, owners))
    shared = halves > 1 and part % (128 * halves) == 0
    share = part // halves if shared else part

    def columns(start):
        return pl.ds(pl.multiple_of(start, share), share)

    def own_share(half):
        return columns(half * share if shared else 0)

    loads = [
        pltpu.make_async_copy(src.at[0], dst, w_sem.at[i])
        for i, (src, dst) in enumerate(((gate_hbm, gate_w), (up_hbm, up_w), (down_hbm, down_w)))
    ]
    for load in loads:
        load.start()

    barrier = pltpu.get_barrier_semaphore()
    for a, b in plane:
        pf, pe = far(a, b)
        pl.semaphore_signal(barrier, inc=1, device_id=(g, pf, pe), device_id_type=MESH)
    for k in range(1, groups):
        pl.semaphore_signal(
            barrier, inc=1, device_id=(lax.rem(g + k, groups), f, e), device_id_type=MESH
        )

    inside, position, diagonal = place(routes[...], owners)
    route_gate = jnp.sum(jnp.where(inside, route_gates[...], 0.0), axis=0, keepdims=True)
    scaled = (column(route_gate, diagonal) * cotangent[...].astype(F32)).astype(BF16)

    slot, fold = folded((owners * ROWS, tokens.shape[0]), 0)
    key = slot + STRIDE * fold
    picks, stacked = [], []
    for chunk in range(OUT_FOLD):
        for which, source in enumerate((tokens[...], scaled)):
            offset = STRIDE * (2 * chunk + which)
            picks.append(jnp.where(key == position + offset, 1.0, 0.0).astype(BF16))
            stacked.append(source[:, chunk * width : (chunk + 1) * width])
    sent = dot(jnp.concatenate(picks, axis=1), jnp.concatenate(stacked, axis=0))
    packed[...] = sent.astype(BF16).reshape(packed.shape)

    pl.semaphore_wait(barrier, len(plane) + groups - 1)
    outs = []
    for i, (a, b) in reversed(list(enumerate(plane))):
        pf, pe = far(a, b)
        copy = pltpu.make_async_remote_copy(
            packed.at[pe], landed.at[f * owners + e], send1.at[i], recv1.at[f * owners + e],
            device_id=(g, pf, pe), device_id_type=MESH,
        )
        copy.start()
        outs.append(copy)
    landed[f * owners + e] = packed[e]

    slot, fold = folded((2 * slots, owners * ROWS), 1)
    chunk_of = jnp.floor(fold * 0.5 + 0.25)
    spot = slot + slots * (fold - 2.0 * chunk_of) + 2 * slots * chunk_of
    at = lax.broadcasted_iota(jnp.int32, spot.shape, 0).astype(F32)
    unpack = [
        jnp.where(spot == at + 2.0 * slots * c, 1.0, 0.0).astype(BF16) for c in range(OUT_FOLD)
    ]
    slot, fold = folded((owners * ROWS, BACK_FOLD * slots), 0)
    at = lax.broadcasted_iota(jnp.int32, slot.shape, 1).astype(F32)
    permute = jnp.where(fold * slots + slot == at, 1.0, 0.0).astype(BF16)

    gate_pre, up_pre, hidden_grad = 0.0, 0.0, 0.0
    for step in range(halves):
        half = lax.rem(f + step, halves)
        for i, (a, b) in enumerate(plane):
            if a == step:
                pf, pe = far(a, b)
                pltpu.make_async_remote_copy(
                    packed.at[pe], landed.at[pf * owners + pe], send1.at[i],
                    recv1.at[pf * owners + pe], device_id=(g, pf, pe), device_id_type=MESH,
                ).wait_recv()
        block = landed[pl.ds(half * owners, owners)].reshape(owners * ROWS, width)
        for chunk in range(OUT_FOLD):
            low = pl.multiple_of(half * quarter + chunk * width, width)
            rows_all[:, pl.ds(low, width)] = dot(unpack[chunk], block).astype(BF16)
        if step == halves - 1:
            for k in range(1, groups):
                d = lax.rem(g + k, groups)
                start = d * part + (f * share if shared else 0)
                copy = pltpu.make_async_remote_copy(
                    rows_all.at[:, columns(start)], slices.at[g, :, own_share(f)],
                    send2.at[k - 1], recv2.at[g], device_id=(d, f, e), device_id_type=MESH,
                )
                copy.start()
                outs.append(copy)
            slices[g] = rows_all[:, pl.ds(pl.multiple_of(g * part, part), part)]
        if step == 0:
            for load in loads:
                load.wait()
        span = pl.ds(pl.multiple_of(half * quarter, quarter), quarter)
        full = rows_all[:, span]
        gate_pre += dot(full, gate_w[span, :])
        up_pre += dot(full, up_w[span, :])
        hidden_grad += dot(full, down_w[:, span], 1, 1)

    gate_pre, up_pre, hidden_grad = gate_pre[:slots], up_pre[:slots], hidden_grad[slots:]
    sigmoid_gate = jax.nn.sigmoid(gate_pre)
    activated = gate_pre * sigmoid_gate
    hidden = activated * up_pre
    gate_grad = hidden_grad * up_pre * sigmoid_gate * (1.0 + gate_pre * (1.0 - sigmoid_gate))
    up_grad = hidden_grad * activated
    mine[...] = jnp.concatenate(
        [
            jnp.concatenate([gate_grad, up_grad], axis=1),
            jnp.concatenate([hidden, jnp.zeros_like(hidden)], axis=1),
        ],
        axis=0,
    ).astype(BF16)
    for k in range(1, groups):
        d = lax.rem(g + k, groups)
        copy = pltpu.make_async_remote_copy(
            mine, factors.at[g], send3.at[k - 1], recv3.at[g],
            device_id=(d, f, e), device_id_type=MESH,
        )
        copy.start()
        outs.append(copy)
    factors[g] = mine[...]

    gate_grad, up_grad = gate_grad.astype(BF16), up_grad.astype(BF16)
    for half in range(halves):
        terms = []
        for chunk in range(BACK_FOLD):
            low = half * quarter + chunk * back_width
            term = dot(gate_grad, gate_w[low : low + back_width, :], 1, 1)
            terms.append(term + dot(up_grad, up_w[low : low + back_width, :], 1, 1))
        ordered = dot(permute, jnp.concatenate(terms, axis=0).astype(BF16))
        back[half * owners : (half + 1) * owners] = ordered.astype(BF16).reshape(
            owners, ROWS, back_width
        )
    for i, (a, b) in enumerate(plane):
        pf, pe = far(a, b)
        copy = pltpu.make_async_remote_copy(
            back.at[pf * owners + pe], returned.at[f * owners + e], send4.at[i],
            recv4.at[f * owners + e], device_id=(g, pf, pe), device_id_type=MESH,
        )
        copy.start()
        outs.append(copy)
    returned[f * owners + e] = back[f * owners + e]

    for k in range(1, groups):
        d = lax.rem(g + k, groups)
        pltpu.make_async_remote_copy(
            rows_all.at[:, columns(0)], slices.at[d, :, own_share(f)], send2.at[k - 1],
            recv2.at[d], device_id=(d, f, e), device_id_type=MESH,
        ).wait_recv()
        if shared:
            for a in range(1, halves):
                pf = lax.rem(f + a, halves)
                copy = pltpu.make_async_remote_copy(
                    slices.at[d, :, own_share(f)], slices.at[d, :, own_share(f)],
                    send5.at[(k - 1) * halves + a], recv5.at[d * halves + f],
                    device_id=(g, pf, e), device_id_type=MESH,
                )
                copy.start()
                outs.append(copy)

    for i, (a, b) in enumerate(plane):
        pf, pe = far(a, b)
        pltpu.make_async_remote_copy(
            back.at[pf * owners + pe], returned.at[pf * owners + pe], send4.at[i],
            recv4.at[pf * owners + pe], device_id=(g, pf, pe), device_id_type=MESH,
        ).wait_recv()
    for k in range(1, groups):
        d = lax.rem(g + k, groups)
        pltpu.make_async_remote_copy(
            mine, factors.at[d], send3.at[k - 1], recv3.at[d],
            device_id=(d, f, e), device_id_type=MESH,
        ).wait_recv()
        if shared:
            for a in range(1, halves):
                pf = lax.rem(f + a, halves)
                pltpu.make_async_remote_copy(
                    slices.at[d, :, own_share(pf)], slices.at[d, :, own_share(pf)],
                    send5.at[(k - 1) * halves + a], recv5.at[d * halves + pf],
                    device_id=(g, pf, e), device_id_type=MESH,
                ).wait_recv()
    for copy in outs:
        copy.wait_send()


def finish(owners, routes, slices, factors, returned, back_key, token_grads, gate_grads, up_grads, down_grads):
    groups, rows, part = slices.shape
    ff = down_grads.shape[1]
    many = groups * rows
    every = slices[...].reshape(many, part)
    top = lax.broadcasted_iota(jnp.int32, factors.shape, 1) < rows // 2
    held = factors[...].astype(F32)
    value = jnp.where(top, held, 0.0).astype(BF16).reshape(many, 2 * ff)
    both = dot(every, value, 0, 0).astype(BF16)
    gate_grads[0] = both[:, :ff]
    up_grads[0] = both[:, ff:]
    value = jnp.where(top, 0.0, held)[:, :, :ff].astype(BF16).reshape(many, ff)
    down_grads[0] = dot(value, every, 0, 0).astype(BF16)

    peers, back_rows, back_width = returned.shape
    come = returned[...].reshape(peers * back_rows, back_width)
    _, position, diagonal = place(routes[...], owners)
    position = column(position, diagonal)
    position = jnp.broadcast_to(position, (position.shape[0], back_key.shape[1]))
    for chunk in range(BACK_FOLD):
        pick = jnp.where(position + STRIDE * chunk == back_key[...], 1.0, 0.0).astype(BF16)
        low = chunk * back_width
        token_grads[:, low : low + back_width] = dot(pick, come).astype(BF16)


def local(groups, halves, owners, tokens, cotangent, routes, route_gates, gate_weight, up_weight, down_weight):
    quarter = tokens.shape[1]
    model, ff = gate_weight.shape[1:]
    slots = owners * CAP
    count = tokens.shape[0]
    part = model // groups
    width, back_width = quarter // OUT_FOLD, quarter // BACK_FOLD
    at = np.arange(owners * ROWS)
    back_chunk, slot = at % ROWS // CAP, at // ROWS * CAP + at % CAP
    back_key = np.tile((slot + STRIDE * back_chunk).astype(np.float32), halves)[None, :]

    vmem = pl.BlockSpec(memory_space=pltpu.VMEM)
    anywhere = pl.BlockSpec(memory_space=pl.ANY)
    peers = halves * owners
    dma = pltpu.SemaphoreType.DMA
    turned = routes.T
    slices, factors, returned = pl.pallas_call(
        functools.partial(kernel, groups, halves, owners),
        out_shape=(
            jax.ShapeDtypeStruct((groups, 2 * slots, part), BF16),
            jax.ShapeDtypeStruct((groups, 2 * slots, 2 * ff), BF16),
            jax.ShapeDtypeStruct((peers, ROWS, back_width), BF16),
        ),
        in_specs=[vmem] * 4 + [anywhere] * 3,
        out_specs=(vmem,) * 3,
        scratch_shapes=[
            pltpu.VMEM((model, ff), BF16),
            pltpu.VMEM((model, ff), BF16),
            pltpu.VMEM((ff, model), BF16),
            pltpu.VMEM((owners, ROWS, width), BF16),
            pltpu.VMEM((peers, ROWS, width), BF16),
            pltpu.VMEM((2 * slots, model), BF16),
            pltpu.VMEM((2 * slots, 2 * ff), BF16),
            pltpu.VMEM((peers, ROWS, back_width), BF16),
            dma((3,)),
            dma((peers,)),
            dma((peers,)),
            dma((groups,)),
            dma((groups,)),
            dma((groups,)),
            dma((groups,)),
            dma((peers,)),
            dma((peers,)),
            dma((groups * halves,)),
            dma((groups * halves,)),
        ],
        compiler_params=pltpu.CompilerParams(
            collective_id=0, has_side_effects=True, vmem_limit_bytes=56 * 1024 * 1024
        ),
    )(
        tokens, cotangent, turned, route_gates.T, gate_weight, up_weight, down_weight,
    )
    return pl.pallas_call(
        functools.partial(finish, owners),
        out_shape=(
            jax.ShapeDtypeStruct((count, quarter), BF16),
            jax.ShapeDtypeStruct((1, part, ff), BF16),
            jax.ShapeDtypeStruct((1, part, ff), BF16),
            jax.ShapeDtypeStruct((1, ff, part), BF16),
        ),
        in_specs=[vmem] * 5,
        out_specs=(vmem,) * 4,
        compiler_params=pltpu.CompilerParams(vmem_limit_bytes=40 * 1024 * 1024),
    )(turned, slices, factors, returned, jnp.asarray(back_key))


def solution(mesh):
    placed = (
        P(("dp", "expert"), "fsdp"),
        P(("dp", "expert"), "fsdp"),
        P(("dp", "expert"), None),
        P(("dp", "expert"), None),
        P("expert", None, "fsdp"),
        P("expert", None, "fsdp"),
        P("expert", "fsdp", None),
    )
    sizes = (mesh.shape["dp"], mesh.shape["fsdp"], mesh.shape["expert"])
    return jax.shard_map(
        functools.partial(local, *sizes),
        mesh=mesh,
        in_specs=placed,
        out_specs=(
            P(("dp", "expert"), "fsdp"),
            P("expert", "dp", "fsdp"),
            P("expert", "dp", "fsdp"),
            P("expert", "fsdp", "dp"),
        ),
        check_vma=False,
    )
```

```python
import functools

import jax
import jax.numpy as jnp
import numpy as np
from jax import lax
from jax.experimental import pallas as pl
from jax.experimental.pallas import tpu as pltpu
from jax.sharding import PartitionSpec as P

CAP = 10
OUT_FOLD = 4
BACK_FOLD = 8
ROWS = 2 * CAP * OUT_FOLD
STRIDE = 4096.0
MESH = pl.DeviceIdType.MESH
F32 = jnp.float32
BF16 = jnp.bfloat16


def dot(a, b, ca=1, cb=0):
    return lax.dot_general(a, b, (((ca,), (cb,)), ((), ())), preferred_element_type=F32)


def place(routes, owners):
    ids = routes.astype(F32)
    inside = ids < float(owners)
    target = jnp.sum(jnp.where(inside, ids, 0.0), axis=0, keepdims=True)
    named = jnp.sum(jnp.where(inside, 1.0, 0.0), axis=0, keepdims=True)
    target = jnp.where(named > 0.0, target, float(owners))
    count = routes.shape[1]
    lanes = lax.broadcasted_iota(jnp.int32, (count, count), 1)
    subs = lax.broadcasted_iota(jnp.int32, (count, count), 0)
    onehot = jnp.where(subs.astype(F32) == target, 1.0, 0.0)
    earlier = jnp.where(subs < lanes, 1.0, 0.0).astype(BF16)
    before = dot(onehot.astype(BF16), earlier)
    position = target * float(CAP) + jnp.sum(before * onehot, axis=0, keepdims=True)
    return inside, position, lanes == subs


def column(row, diagonal):
    return jnp.sum(jnp.where(diagonal, row, 0.0), axis=1, keepdims=True)


def folded(shape, axis):
    at = lax.broadcasted_iota(jnp.int32, shape, axis).astype(F32)
    owner = jnp.floor((at + 0.5) * (1.0 / ROWS))
    at = at - owner * ROWS
    fold = jnp.floor((at + 0.5) * (1.0 / CAP))
    return owner * CAP + (at - fold * CAP), fold


def kernel(
    groups, halves, owners,
    tokens, cotangent, routes, route_gates, gate_hbm, up_hbm, down_hbm,
    slices, factors, returned,
    gate_w, up_w, down_w, packed, landed, rows_all, mine, back,
    w_sem, send1, recv1, send2, recv2, send3, recv3, send4, recv4, send5, recv5,
):
    g, f, e = lax.axis_index("dp"), lax.axis_index("fsdp"), lax.axis_index("expert")
    slots = owners * CAP
    quarter = tokens.shape[1]
    width = quarter // OUT_FOLD
    back_width = quarter // BACK_FOLD
    part = slices.shape[2]
    plane = [(a, b) for a in range(halves) for b in range(owners) if (a, b) != (0, 0)]
    far = lambda a, b: (lax.rem(f + a, halves), lax.rem(e + b, owners))
    shared = halves > 1 and part % (128 * halves) == 0
    share = part // halves if shared else part

    def columns(start):
        return pl.ds(pl.multiple_of(start, share), share)

    def own_share(half):
        return columns(half * share if shared else 0)

    loads = [
        pltpu.make_async_copy(src.at[0], dst, w_sem.at[i])
        for i, (src, dst) in enumerate(((gate_hbm, gate_w), (up_hbm, up_w), (down_hbm, down_w)))
    ]
    for load in loads:
        load.start()

    barrier = pltpu.get_barrier_semaphore()
    for a, b in plane:
        pf, pe = far(a, b)
        pl.semaphore_signal(barrier, inc=1, device_id=(g, pf, pe), device_id_type=MESH)
    for k in range(1, groups):
        pl.semaphore_signal(
            barrier, inc=1, device_id=(lax.rem(g + k, groups), f, e), device_id_type=MESH
        )

    inside, position, diagonal = place(routes[...], owners)
    route_gate = jnp.sum(jnp.where(inside, route_gates[...], 0.0), axis=0, keepdims=True)
    scaled = (column(route_gate, diagonal) * cotangent[...].astype(F32)).astype(BF16)

    slot, fold = folded((owners * ROWS, tokens.shape[0]), 0)
    key = slot + STRIDE * fold
    picks, stacked = [], []
    for chunk in range(OUT_FOLD):
        for which, source in enumerate((tokens[...], scaled)):
            offset = STRIDE * (2 * chunk + which)
            picks.append(jnp.where(key == position + offset, 1.0, 0.0).astype(BF16))
            stacked.append(source[:, chunk * width : (chunk + 1) * width])
    sent = dot(jnp.concatenate(picks, axis=1), jnp.concatenate(stacked, axis=0))
    packed[...] = sent.astype(BF16).reshape(packed.shape)

    pl.semaphore_wait(barrier, len(plane) + groups - 1)
    outs = []
    for i, (a, b) in reversed(list(enumerate(plane))):
        pf, pe = far(a, b)
        copy = pltpu.make_async_remote_copy(
            packed.at[pe], landed.at[f * owners + e], send1.at[i], recv1.at[f * owners + e],
            device_id=(g, pf, pe), device_id_type=MESH,
        )
        copy.start()
        outs.append(copy)
    landed[f * owners + e] = packed[e]

    slot, fold = folded((2 * slots, owners * ROWS), 1)
    chunk_of = jnp.floor(fold * 0.5 + 0.25)
    spot = slot + slots * (fold - 2.0 * chunk_of) + 2 * slots * chunk_of
    at = lax.broadcasted_iota(jnp.int32, spot.shape, 0).astype(F32)
    unpack = [
        jnp.where(spot == at + 2.0 * slots * c, 1.0, 0.0).astype(BF16) for c in range(OUT_FOLD)
    ]
    slot, fold = folded((owners * ROWS, BACK_FOLD * slots), 0)
    at = lax.broadcasted_iota(jnp.int32, slot.shape, 1).astype(F32)
    permute = jnp.where(fold * slots + slot == at, 1.0, 0.0).astype(BF16)

    gate_pre, up_pre, hidden_grad = 0.0, 0.0, 0.0
    for step in range(halves):
        half = lax.rem(f + step, halves)
        for i, (a, b) in enumerate(plane):
            if a == step:
                pf, pe = far(a, b)
                pltpu.make_async_remote_copy(
                    packed.at[pe], landed.at[pf * owners + pe], send1.at[i],
                    recv1.at[pf * owners + pe], device_id=(g, pf, pe), device_id_type=MESH,
                ).wait_recv()
        block = landed[pl.ds(half * owners, owners)].reshape(owners * ROWS, width)
        for chunk in range(OUT_FOLD):
            low = pl.multiple_of(half * quarter + chunk * width, width)
            rows_all[:, pl.ds(low, width)] = dot(unpack[chunk], block).astype(BF16)
        if step == halves - 1:
            for k in range(1, groups):
                d = lax.rem(g + k, groups)
                start = d * part + (f * share if shared else 0)
                copy = pltpu.make_async_remote_copy(
                    rows_all.at[:, columns(start)], slices.at[g, :, own_share(f)],
                    send2.at[k - 1], recv2.at[g], device_id=(d, f, e), device_id_type=MESH,
                )
                copy.start()
                outs.append(copy)
            slices[g] = rows_all[:, pl.ds(pl.multiple_of(g * part, part), part)]
        if step == 0:
            for load in loads:
                load.wait()
        span = pl.ds(pl.multiple_of(half * quarter, quarter), quarter)
        full = rows_all[:, span]
        gate_pre += dot(full, gate_w[span, :])
        up_pre += dot(full, up_w[span, :])
        hidden_grad += dot(full, down_w[:, span], 1, 1)

    gate_pre, up_pre, hidden_grad = gate_pre[:slots], up_pre[:slots], hidden_grad[slots:]
    sigmoid_gate = jax.nn.sigmoid(gate_pre)
    activated = gate_pre * sigmoid_gate
    hidden = activated * up_pre
    gate_grad = hidden_grad * up_pre * sigmoid_gate * (1.0 + gate_pre * (1.0 - sigmoid_gate))
    up_grad = hidden_grad * activated
    mine[...] = jnp.concatenate(
        [
            jnp.concatenate([gate_grad, up_grad], axis=1),
            jnp.concatenate([hidden, jnp.zeros_like(hidden)], axis=1),
        ],
        axis=0,
    ).astype(BF16)
    for k in range(1, groups):
        d = lax.rem(g + k, groups)
        copy = pltpu.make_async_remote_copy(
            mine, factors.at[g], send3.at[k - 1], recv3.at[g],
            device_id=(d, f, e), device_id_type=MESH,
        )
        copy.start()
        outs.append(copy)
    factors[g] = mine[...]

    gate_grad, up_grad = gate_grad.astype(BF16), up_grad.astype(BF16)
    for half in range(halves):
        terms = []
        for chunk in range(BACK_FOLD):
            low = half * quarter + chunk * back_width
            term = dot(gate_grad, gate_w[low : low + back_width, :], 1, 1)
            terms.append(term + dot(up_grad, up_w[low : low + back_width, :], 1, 1))
        ordered = dot(permute, jnp.concatenate(terms, axis=0).astype(BF16))
        back[half * owners : (half + 1) * owners] = ordered.astype(BF16).reshape(
            owners, ROWS, back_width
        )
    for i, (a, b) in enumerate(plane):
        pf, pe = far(a, b)
        copy = pltpu.make_async_remote_copy(
            back.at[pf * owners + pe], returned.at[f * owners + e], send4.at[i],
            recv4.at[f * owners + e], device_id=(g, pf, pe), device_id_type=MESH,
        )
        copy.start()
        outs.append(copy)
    returned[f * owners + e] = back[f * owners + e]

    for k in range(1, groups):
        d = lax.rem(g + k, groups)
        pltpu.make_async_remote_copy(
            rows_all.at[:, columns(0)], slices.at[d, :, own_share(f)], send2.at[k - 1],
            recv2.at[d], device_id=(d, f, e), device_id_type=MESH,
        ).wait_recv()
        if shared:
            for a in range(1, halves):
                pf = lax.rem(f + a, halves)
                copy = pltpu.make_async_remote_copy(
                    slices.at[d, :, own_share(f)], slices.at[d, :, own_share(f)],
                    send5.at[(k - 1) * halves + a], recv5.at[d * halves + f],
                    device_id=(g, pf, e), device_id_type=MESH,
                )
                copy.start()
                outs.append(copy)

    for i, (a, b) in enumerate(plane):
        pf, pe = far(a, b)
        pltpu.make_async_remote_copy(
            back.at[pf * owners + pe], returned.at[pf * owners + pe], send4.at[i],
            recv4.at[pf * owners + pe], device_id=(g, pf, pe), device_id_type=MESH,
        ).wait_recv()
    for k in range(1, groups):
        d = lax.rem(g + k, groups)
        pltpu.make_async_remote_copy(
            mine, factors.at[d], send3.at[k - 1], recv3.at[d],
            device_id=(d, f, e), device_id_type=MESH,
        ).wait_recv()
        if shared:
            for a in range(1, halves):
                pf = lax.rem(f + a, halves)
                pltpu.make_async_remote_copy(
                    slices.at[d, :, own_share(pf)], slices.at[d, :, own_share(pf)],
                    send5.at[(k - 1) * halves + a], recv5.at[d * halves + pf],
                    device_id=(g, pf, e), device_id_type=MESH,
                ).wait_recv()
    for copy in outs:
        copy.wait_send()


def finish(
    owners, routes, slices_hbm, factors_hbm, returned_hbm, back_key, token_out, gate_out, up_out, down_out,
    slices, factors, returned, token_grads, gate_grads, up_grads, down_grads, in_sem, out_sem,
):
    loads = [
        pltpu.make_async_copy(src, dst, in_sem.at[i])
        for i, (src, dst) in enumerate(
            ((returned_hbm, returned), (slices_hbm, slices), (factors_hbm, factors))
        )
    ]
    for load in loads:
        load.start()
    stores = [
        pltpu.make_async_copy(src, dst, out_sem.at[i])
        for i, (src, dst) in enumerate((
            (token_grads, token_out), (gate_grads, gate_out.at[0]), (up_grads, up_out.at[0]),
            (down_grads, down_out.at[0]),
        ))
    ]
    _, position, diagonal = place(routes[...], owners)
    position = column(position, diagonal)
    position = jnp.broadcast_to(position, (position.shape[0], back_key.shape[1]))
    peers, back_rows, back_width = returned.shape
    loads[0].wait()
    come = returned[...].reshape(peers * back_rows, back_width)
    for chunk in range(BACK_FOLD):
        pick = jnp.where(position + STRIDE * chunk == back_key[...], 1.0, 0.0).astype(BF16)
        low = chunk * back_width
        token_grads[:, low : low + back_width] = dot(pick, come).astype(BF16)
    stores[0].start()

    loads[1].wait()
    loads[2].wait()
    groups, rows, part = slices.shape
    ff = down_grads.shape[0]
    many = groups * rows
    every = slices[...].reshape(many, part)
    top = lax.broadcasted_iota(jnp.int32, factors.shape, 1) < rows // 2
    held = factors[...].astype(F32)
    value = jnp.where(top, held, 0.0).astype(BF16).reshape(many, 2 * ff)
    both = dot(every, value, 0, 0).astype(BF16)
    gate_grads[...] = both[:, :ff]
    up_grads[...] = both[:, ff:]
    stores[1].start()
    stores[2].start()
    value = jnp.where(top, 0.0, held)[:, :, :ff].astype(BF16).reshape(many, ff)
    down_grads[...] = dot(value, every, 0, 0).astype(BF16)
    stores[3].start()
    for store in stores:
        store.wait()


def local(groups, halves, owners, tokens, cotangent, routes, route_gates, gate_weight, up_weight, down_weight):
    quarter = tokens.shape[1]
    model, ff = gate_weight.shape[1:]
    slots = owners * CAP
    count = tokens.shape[0]
    part = model // groups
    width, back_width = quarter // OUT_FOLD, quarter // BACK_FOLD
    at = np.arange(owners * ROWS)
    back_chunk, slot = at % ROWS // CAP, at // ROWS * CAP + at % CAP
    back_key = np.tile((slot + STRIDE * back_chunk).astype(np.float32), halves)[None, :]

    vmem = pl.BlockSpec(memory_space=pltpu.VMEM)
    anywhere = pl.BlockSpec(memory_space=pl.ANY)
    peers = halves * owners
    dma = pltpu.SemaphoreType.DMA
    turned = routes.T
    slices, factors, returned = pl.pallas_call(
        functools.partial(kernel, groups, halves, owners),
        out_shape=(
            jax.ShapeDtypeStruct((groups, 2 * slots, part), BF16),
            jax.ShapeDtypeStruct((groups, 2 * slots, 2 * ff), BF16),
            jax.ShapeDtypeStruct((peers, ROWS, back_width), BF16),
        ),
        in_specs=[vmem] * 4 + [anywhere] * 3,
        out_specs=(vmem,) * 3,
        scratch_shapes=[
            pltpu.VMEM((model, ff), BF16),
            pltpu.VMEM((model, ff), BF16),
            pltpu.VMEM((ff, model), BF16),
            pltpu.VMEM((owners, ROWS, width), BF16),
            pltpu.VMEM((peers, ROWS, width), BF16),
            pltpu.VMEM((2 * slots, model), BF16),
            pltpu.VMEM((2 * slots, 2 * ff), BF16),
            pltpu.VMEM((peers, ROWS, back_width), BF16),
            dma((3,)),
            dma((peers,)),
            dma((peers,)),
            dma((groups,)),
            dma((groups,)),
            dma((groups,)),
            dma((groups,)),
            dma((peers,)),
            dma((peers,)),
            dma((groups * halves,)),
            dma((groups * halves,)),
        ],
        compiler_params=pltpu.CompilerParams(
            collective_id=0, has_side_effects=True, vmem_limit_bytes=56 * 1024 * 1024
        ),
    )(
        tokens, cotangent, turned, route_gates.T, gate_weight, up_weight, down_weight,
    )
    return pl.pallas_call(
        functools.partial(finish, owners),
        out_shape=(
            jax.ShapeDtypeStruct((count, quarter), BF16),
            jax.ShapeDtypeStruct((1, part, ff), BF16),
            jax.ShapeDtypeStruct((1, part, ff), BF16),
            jax.ShapeDtypeStruct((1, ff, part), BF16),
        ),
        in_specs=[vmem] + [pl.BlockSpec(memory_space=pltpu.HBM)] * 3 + [vmem],
        out_specs=(pl.BlockSpec(memory_space=pltpu.HBM),) * 4,
        scratch_shapes=[
            pltpu.VMEM((groups, 2 * slots, part), BF16),
            pltpu.VMEM((groups, 2 * slots, 2 * ff), BF16),
            pltpu.VMEM((peers, ROWS, back_width), BF16),
            pltpu.VMEM((count, quarter), BF16),
            pltpu.VMEM((part, ff), BF16),
            pltpu.VMEM((part, ff), BF16),
            pltpu.VMEM((ff, part), BF16),
            dma((3,)),
            dma((4,)),
        ],
        compiler_params=pltpu.CompilerParams(vmem_limit_bytes=56 * 1024 * 1024),
    )(turned, slices, factors, returned, jnp.asarray(back_key))


def solution(mesh):
    placed = (
        P(("dp", "expert"), "fsdp"),
        P(("dp", "expert"), "fsdp"),
        P(("dp", "expert"), None),
        P(("dp", "expert"), None),
        P("expert", None, "fsdp"),
        P("expert", None, "fsdp"),
        P("expert", "fsdp", None),
    )
    sizes = (mesh.shape["dp"], mesh.shape["fsdp"], mesh.shape["expert"])
    return jax.shard_map(
        functools.partial(local, *sizes),
        mesh=mesh,
        in_specs=placed,
        out_specs=(
            P(("dp", "expert"), "fsdp"),
            P("expert", "dp", "fsdp"),
            P("expert", "dp", "fsdp"),
            P("expert", "fsdp", "dp"),
        ),
        check_vma=False,
    )
```

```python
import functools

import jax
import jax.numpy as jnp
import numpy as np
from jax import lax
from jax.experimental import pallas as pl
from jax.experimental.pallas import tpu as pltpu
from jax.sharding import PartitionSpec as P

CAP = 10
OUT_FOLD = 4
BACK_FOLD = 8
ROWS = 2 * CAP * OUT_FOLD
STRIDE = 4096.0
MESH = pl.DeviceIdType.MESH
F32 = jnp.float32
BF16 = jnp.bfloat16


def dot(a, b, ca=1, cb=0):
    return lax.dot_general(a, b, (((ca,), (cb,)), ((), ())), preferred_element_type=F32)


def up_split(ff):
    return ff // 3 * 2 if ff % 384 == 0 else ff


def place(routes, owners):
    ids = routes.astype(F32)
    inside = ids < float(owners)
    target = jnp.sum(jnp.where(inside, ids, 0.0), axis=0, keepdims=True)
    named = jnp.sum(jnp.where(inside, 1.0, 0.0), axis=0, keepdims=True)
    target = jnp.where(named > 0.0, target, float(owners))
    count = routes.shape[1]
    lanes = lax.broadcasted_iota(jnp.int32, (count, count), 1)
    subs = lax.broadcasted_iota(jnp.int32, (count, count), 0)
    onehot = jnp.where(subs.astype(F32) == target, 1.0, 0.0)
    earlier = jnp.where(subs < lanes, 1.0, 0.0).astype(BF16)
    before = dot(onehot.astype(BF16), earlier)
    position = target * float(CAP) + jnp.sum(before * onehot, axis=0, keepdims=True)
    return inside, position, lanes == subs


def column(row, diagonal):
    return jnp.sum(jnp.where(diagonal, row, 0.0), axis=1, keepdims=True)


def folded(shape, axis):
    at = lax.broadcasted_iota(jnp.int32, shape, axis).astype(F32)
    owner = jnp.floor((at + 0.5) * (1.0 / ROWS))
    at = at - owner * ROWS
    fold = jnp.floor((at + 0.5) * (1.0 / CAP))
    return owner * CAP + (at - fold * CAP), fold


def kernel(
    groups, halves, owners,
    tokens, cotangent, routes, route_gates, gate_hbm, up_hbm, down_hbm,
    slices, factors, returned,
    gate_w, up_w, down_w, packed, landed, rows_all, mine, back,
    w_sem, send1, recv1, send2, recv2, send3, recv3, send4, recv4, send5, recv5,
):
    g, f, e = lax.axis_index("dp"), lax.axis_index("fsdp"), lax.axis_index("expert")
    slots = owners * CAP
    quarter = tokens.shape[1]
    width = quarter // OUT_FOLD
    back_width = quarter // BACK_FOLD
    part = slices.shape[2]
    plane = [(a, b) for a in range(halves) for b in range(owners) if (a, b) != (0, 0)]
    far = lambda a, b: (lax.rem(f + a, halves), lax.rem(e + b, owners))
    shared = halves > 1 and part % (128 * halves) == 0
    share = part // halves if shared else part

    def columns(start):
        return pl.ds(pl.multiple_of(start, share), share)

    def own_share(half):
        return columns(half * share if shared else 0)

    loads = [
        pltpu.make_async_copy(src.at[0], dst, w_sem.at[i])
        for i, (src, dst) in enumerate(((gate_hbm, gate_w), (up_hbm, up_w), (down_hbm, down_w)))
    ]
    for load in loads:
        load.start()

    barrier = pltpu.get_barrier_semaphore()
    for a, b in plane:
        pf, pe = far(a, b)
        pl.semaphore_signal(barrier, inc=1, device_id=(g, pf, pe), device_id_type=MESH)
    for k in range(1, groups):
        pl.semaphore_signal(
            barrier, inc=1, device_id=(lax.rem(g + k, groups), f, e), device_id_type=MESH
        )

    inside, position, diagonal = place(routes[...], owners)
    route_gate = jnp.sum(jnp.where(inside, route_gates[...], 0.0), axis=0, keepdims=True)
    scaled = (column(route_gate, diagonal) * cotangent[...].astype(F32)).astype(BF16)

    slot, fold = folded((owners * ROWS, tokens.shape[0]), 0)
    key = slot + STRIDE * fold
    picks, stacked = [], []
    for chunk in range(OUT_FOLD):
        for which, source in enumerate((tokens[...], scaled)):
            offset = STRIDE * (2 * chunk + which)
            picks.append(jnp.where(key == position + offset, 1.0, 0.0).astype(BF16))
            stacked.append(source[:, chunk * width : (chunk + 1) * width])
    sent = dot(jnp.concatenate(picks, axis=1), jnp.concatenate(stacked, axis=0))
    packed[...] = sent.astype(BF16).reshape(packed.shape)

    pl.semaphore_wait(barrier, len(plane) + groups - 1)
    outs = []
    for i, (a, b) in reversed(list(enumerate(plane))):
        pf, pe = far(a, b)
        copy = pltpu.make_async_remote_copy(
            packed.at[pe], landed.at[f * owners + e], send1.at[i], recv1.at[f * owners + e],
            device_id=(g, pf, pe), device_id_type=MESH,
        )
        copy.start()
        outs.append(copy)
    landed[f * owners + e] = packed[e]

    slot, fold = folded((2 * slots, owners * ROWS), 1)
    chunk_of = jnp.floor(fold * 0.5 + 0.25)
    spot = slot + slots * (fold - 2.0 * chunk_of) + 2 * slots * chunk_of
    at = lax.broadcasted_iota(jnp.int32, spot.shape, 0).astype(F32)
    unpack = [
        jnp.where(spot == at + 2.0 * slots * c, 1.0, 0.0).astype(BF16) for c in range(OUT_FOLD)
    ]
    slot, fold = folded((owners * ROWS, BACK_FOLD * slots), 0)
    at = lax.broadcasted_iota(jnp.int32, slot.shape, 1).astype(F32)
    permute = jnp.where(fold * slots + slot == at, 1.0, 0.0).astype(BF16)

    gate_pre, up_pre, hidden_grad = 0.0, 0.0, 0.0
    for step in range(halves):
        half = lax.rem(f + step, halves)
        for i, (a, b) in enumerate(plane):
            if a == step:
                pf, pe = far(a, b)
                pltpu.make_async_remote_copy(
                    packed.at[pe], landed.at[pf * owners + pe], send1.at[i],
                    recv1.at[pf * owners + pe], device_id=(g, pf, pe), device_id_type=MESH,
                ).wait_recv()
        block = landed[pl.ds(half * owners, owners)].reshape(owners * ROWS, width)
        for chunk in range(OUT_FOLD):
            low = pl.multiple_of(half * quarter + chunk * width, width)
            rows_all[:, pl.ds(low, width)] = dot(unpack[chunk], block).astype(BF16)
        if step == halves - 1:
            for k in range(1, groups):
                d = lax.rem(g + k, groups)
                start = d * part + (f * share if shared else 0)
                copy = pltpu.make_async_remote_copy(
                    rows_all.at[:, columns(start)], slices.at[g, :, own_share(f)],
                    send2.at[k - 1], recv2.at[g], device_id=(d, f, e), device_id_type=MESH,
                )
                copy.start()
                outs.append(copy)
            slices[g] = rows_all[:, pl.ds(pl.multiple_of(g * part, part), part)]
        if step == 0:
            for load in loads:
                load.wait()
        span = pl.ds(pl.multiple_of(half * quarter, quarter), quarter)
        full = rows_all[:, span]
        gate_pre += dot(full, gate_w[span, :])
        up_pre += dot(full, up_w[span, :])
        hidden_grad += dot(full, down_w[:, span], 1, 1)

    gate_pre, up_pre, hidden_grad = gate_pre[:slots], up_pre[:slots], hidden_grad[slots:]
    sigmoid_gate = jax.nn.sigmoid(gate_pre)
    activated = gate_pre * sigmoid_gate
    hidden = activated * up_pre
    gate_grad = hidden_grad * up_pre * sigmoid_gate * (1.0 + gate_pre * (1.0 - sigmoid_gate))
    up_grad = hidden_grad * activated
    split = up_split(hidden.shape[1])
    rest = hidden.shape[1] - split
    beside = [hidden] + ([up_grad[:, split:]] if rest else [])
    beside.append(jnp.zeros((slots, split - rest), F32))
    mine[...] = jnp.concatenate(
        [
            jnp.concatenate([gate_grad, up_grad[:, :split]], axis=1),
            jnp.concatenate(beside, axis=1),
        ],
        axis=0,
    ).astype(BF16)
    for k in range(1, groups):
        d = lax.rem(g + k, groups)
        copy = pltpu.make_async_remote_copy(
            mine, factors.at[g], send3.at[k - 1], recv3.at[g],
            device_id=(d, f, e), device_id_type=MESH,
        )
        copy.start()
        outs.append(copy)
    factors[g] = mine[...]

    gate_grad, up_grad = gate_grad.astype(BF16), up_grad.astype(BF16)
    for half in range(halves):
        terms = []
        for chunk in range(BACK_FOLD):
            low = half * quarter + chunk * back_width
            term = dot(gate_grad, gate_w[low : low + back_width, :], 1, 1)
            terms.append(term + dot(up_grad, up_w[low : low + back_width, :], 1, 1))
        ordered = dot(permute, jnp.concatenate(terms, axis=0).astype(BF16))
        back[half * owners : (half + 1) * owners] = ordered.astype(BF16).reshape(
            owners, ROWS, back_width
        )
    for i, (a, b) in enumerate(plane):
        pf, pe = far(a, b)
        copy = pltpu.make_async_remote_copy(
            back.at[pf * owners + pe], returned.at[f * owners + e], send4.at[i],
            recv4.at[f * owners + e], device_id=(g, pf, pe), device_id_type=MESH,
        )
        copy.start()
        outs.append(copy)
    returned[f * owners + e] = back[f * owners + e]

    for k in range(1, groups):
        d = lax.rem(g + k, groups)
        pltpu.make_async_remote_copy(
            rows_all.at[:, columns(0)], slices.at[d, :, own_share(f)], send2.at[k - 1],
            recv2.at[d], device_id=(d, f, e), device_id_type=MESH,
        ).wait_recv()
        if shared:
            for a in range(1, halves):
                pf = lax.rem(f + a, halves)
                copy = pltpu.make_async_remote_copy(
                    slices.at[d, :, own_share(f)], slices.at[d, :, own_share(f)],
                    send5.at[(k - 1) * halves + a], recv5.at[d * halves + f],
                    device_id=(g, pf, e), device_id_type=MESH,
                )
                copy.start()
                outs.append(copy)

    for i, (a, b) in enumerate(plane):
        pf, pe = far(a, b)
        pltpu.make_async_remote_copy(
            back.at[pf * owners + pe], returned.at[pf * owners + pe], send4.at[i],
            recv4.at[pf * owners + pe], device_id=(g, pf, pe), device_id_type=MESH,
        ).wait_recv()
    for k in range(1, groups):
        d = lax.rem(g + k, groups)
        pltpu.make_async_remote_copy(
            mine, factors.at[d], send3.at[k - 1], recv3.at[d],
            device_id=(d, f, e), device_id_type=MESH,
        ).wait_recv()
        if shared:
            for a in range(1, halves):
                pf = lax.rem(f + a, halves)
                pltpu.make_async_remote_copy(
                    slices.at[d, :, own_share(pf)], slices.at[d, :, own_share(pf)],
                    send5.at[(k - 1) * halves + a], recv5.at[d * halves + pf],
                    device_id=(g, pf, e), device_id_type=MESH,
                ).wait_recv()
    for copy in outs:
        copy.wait_send()


def finish(
    owners, routes, slices_hbm, factors_hbm, returned_hbm, back_key, token_out, gate_out, up_out, down_out,
    slices, factors, returned, token_grads, gate_grads, up_grads, down_grads, in_sem, out_sem,
):
    loads = [
        pltpu.make_async_copy(src, dst, in_sem.at[i])
        for i, (src, dst) in enumerate(
            ((returned_hbm, returned), (slices_hbm, slices), (factors_hbm, factors))
        )
    ]
    for load in loads:
        load.start()
    stores = [
        pltpu.make_async_copy(src, dst, out_sem.at[i])
        for i, (src, dst) in enumerate((
            (token_grads, token_out), (gate_grads, gate_out.at[0]), (up_grads, up_out.at[0]),
            (down_grads, down_out.at[0]),
        ))
    ]
    _, position, diagonal = place(routes[...], owners)
    position = column(position, diagonal)
    position = jnp.broadcast_to(position, (position.shape[0], back_key.shape[1]))
    peers, back_rows, back_width = returned.shape
    loads[0].wait()
    come = returned[...].reshape(peers * back_rows, back_width)
    for chunk in range(BACK_FOLD):
        pick = jnp.where(position + STRIDE * chunk == back_key[...], 1.0, 0.0).astype(BF16)
        low = chunk * back_width
        token_grads[:, low : low + back_width] = dot(pick, come).astype(BF16)
    stores[0].start()

    loads[1].wait()
    loads[2].wait()
    groups, rows, part = slices.shape
    ff = down_grads.shape[0]
    many = groups * rows
    every = slices[...].reshape(many, part)
    top = lax.broadcasted_iota(jnp.int32, factors.shape, 1) < rows // 2
    held = factors[...].astype(F32)
    value = jnp.where(top, held, 0.0)
    rest = 2 * ff - held.shape[2]
    if rest:
        moved = held[:, rows // 2 :, ff : ff + rest]
        moved = jnp.concatenate([moved, jnp.zeros_like(moved)], axis=1)
        value = jnp.concatenate([value, moved], axis=2)
    value = value.astype(BF16).reshape(many, 2 * ff)
    both = dot(every, value, 0, 0).astype(BF16)
    gate_grads[...] = both[:, :ff]
    up_grads[...] = both[:, ff:]
    stores[1].start()
    stores[2].start()
    value = jnp.where(top, 0.0, held)[:, :, :ff].astype(BF16).reshape(many, ff)
    down_grads[...] = dot(value, every, 0, 0).astype(BF16)
    stores[3].start()
    for store in stores:
        store.wait()


def local(groups, halves, owners, tokens, cotangent, routes, route_gates, gate_weight, up_weight, down_weight):
    quarter = tokens.shape[1]
    model, ff = gate_weight.shape[1:]
    slots = owners * CAP
    count = tokens.shape[0]
    part = model // groups
    width, back_width = quarter // OUT_FOLD, quarter // BACK_FOLD
    at = np.arange(owners * ROWS)
    back_chunk, slot = at % ROWS // CAP, at // ROWS * CAP + at % CAP
    back_key = np.tile((slot + STRIDE * back_chunk).astype(np.float32), halves)[None, :]

    vmem = pl.BlockSpec(memory_space=pltpu.VMEM)
    anywhere = pl.BlockSpec(memory_space=pl.ANY)
    peers = halves * owners
    dma = pltpu.SemaphoreType.DMA
    turned = routes.T
    slices, factors, returned = pl.pallas_call(
        functools.partial(kernel, groups, halves, owners),
        out_shape=(
            jax.ShapeDtypeStruct((groups, 2 * slots, part), BF16),
            jax.ShapeDtypeStruct((groups, 2 * slots, ff + up_split(ff)), BF16),
            jax.ShapeDtypeStruct((peers, ROWS, back_width), BF16),
        ),
        in_specs=[vmem] * 4 + [anywhere] * 3,
        out_specs=(vmem,) * 3,
        scratch_shapes=[
            pltpu.VMEM((model, ff), BF16),
            pltpu.VMEM((model, ff), BF16),
            pltpu.VMEM((ff, model), BF16),
            pltpu.VMEM((owners, ROWS, width), BF16),
            pltpu.VMEM((peers, ROWS, width), BF16),
            pltpu.VMEM((2 * slots, model), BF16),
            pltpu.VMEM((2 * slots, ff + up_split(ff)), BF16),
            pltpu.VMEM((peers, ROWS, back_width), BF16),
            dma((3,)),
            dma((peers,)),
            dma((peers,)),
            dma((groups,)),
            dma((groups,)),
            dma((groups,)),
            dma((groups,)),
            dma((peers,)),
            dma((peers,)),
            dma((groups * halves,)),
            dma((groups * halves,)),
        ],
        compiler_params=pltpu.CompilerParams(
            collective_id=0, has_side_effects=True, vmem_limit_bytes=56 * 1024 * 1024
        ),
    )(
        tokens, cotangent, turned, route_gates.T, gate_weight, up_weight, down_weight,
    )
    return pl.pallas_call(
        functools.partial(finish, owners),
        out_shape=(
            jax.ShapeDtypeStruct((count, quarter), BF16),
            jax.ShapeDtypeStruct((1, part, ff), BF16),
            jax.ShapeDtypeStruct((1, part, ff), BF16),
            jax.ShapeDtypeStruct((1, ff, part), BF16),
        ),
        in_specs=[vmem] + [pl.BlockSpec(memory_space=pltpu.HBM)] * 3 + [vmem],
        out_specs=(pl.BlockSpec(memory_space=pltpu.HBM),) * 4,
        scratch_shapes=[
            pltpu.VMEM((groups, 2 * slots, part), BF16),
            pltpu.VMEM((groups, 2 * slots, ff + up_split(ff)), BF16),
            pltpu.VMEM((peers, ROWS, back_width), BF16),
            pltpu.VMEM((count, quarter), BF16),
            pltpu.VMEM((part, ff), BF16),
            pltpu.VMEM((part, ff), BF16),
            pltpu.VMEM((ff, part), BF16),
            dma((3,)),
            dma((4,)),
        ],
        compiler_params=pltpu.CompilerParams(vmem_limit_bytes=56 * 1024 * 1024),
    )(turned, slices, factors, returned, jnp.asarray(back_key))


def solution(mesh):
    placed = (
        P(("dp", "expert"), "fsdp"),
        P(("dp", "expert"), "fsdp"),
        P(("dp", "expert"), None),
        P(("dp", "expert"), None),
        P("expert", None, "fsdp"),
        P("expert", None, "fsdp"),
        P("expert", "fsdp", None),
    )
    sizes = (mesh.shape["dp"], mesh.shape["fsdp"], mesh.shape["expert"])
    return jax.shard_map(
        functools.partial(local, *sizes),
        mesh=mesh,
        in_specs=placed,
        out_specs=(
            P(("dp", "expert"), "fsdp"),
            P("expert", "dp", "fsdp"),
            P("expert", "dp", "fsdp"),
            P("expert", "fsdp", "dp"),
        ),
        check_vma=False,
    )
```
